32 devices in a mesh: state: 16 (over z, y, core), grid: 2 (over x).
Axes of the slice: x: 2, y: 2, z: 4, core: 2. Of those that a mesh axis runs over, the one named last changes fastest.
Arguments:
- orbitals: bfloat16 [64, 32, 3584], P('state', 'grid'), may hold values from -6 to 6
- first_rotation: bfloat16 [64, 64], P(None, 'state'), may hold values from -0.75 to 0.75
- second_rotation: bfloat16 [64, 64], P(None, 'state'), may hold values from -0.75 to 0.75
- occupancy: bfloat16 [64], P('state'), may hold values from 0.1 to 6, as said below
- local_potential: float32 [32, 3584], P('grid'), may hold values from -2 to 0.5
Outputs:
- new_images: bfloat16 [64, 32, 3584], P('state', 'grid')
- density: float32 [32, 3584], P('grid')
The draws below stay inside these ranges and needn't reach their ends.
Inputs may be any that keep to these rules, and one draw needn't show every extreme that they name: `occupancy`: positive occupations.
All inputs are finite; a program needn't handle non-finite values.
Results may differ from the reference program's by a relative error of at most 0.018.
Values may be sent and summed in bfloat16 or wider, within the bound.
A program may use at most 128 MiB of HBM per device.

```python
import jax
import jax.numpy as jnp
from jax import lax

GY = 224
GZ = 16
RADIUS = 6
NS = 64
NX = 32
GYZ = 3584


def draw_occupancy(key, part):
    position = jnp.arange(NS, dtype=jnp.float32) / NS
    base_level = 2.0 * jnp.exp(-1.2 * position)
    factor = jax.random.uniform(key, (NS,), jnp.float32, 0.6, 1.4)
    return (base_level * factor).astype(jnp.bfloat16)


def block_levels(key, dims, split, smallest, largest):
    def one(dim, parts):
        heights = jax.random.uniform(jax.random.fold_in(jax.random.fold_in(key, 6), dim), (parts,), jnp.float32, smallest / len(split), largest / len(split))
        return jnp.repeat(jnp.exp(heights), dims[dim] // parts).reshape((-1,) + (1,) * (len(dims) - dim - 1))

    loudness = one(*split[0])
    for cut in split[1:]:
        loudness = loudness * one(*cut)
    return loudness


def scatter_about(own_key, shape, width, most, cuts=(), held_as=jnp.bfloat16):
    level = block_levels(own_key, shape, cuts, -0.22, 0.18) if cuts else 1.0
    array = jax.random.normal(own_key, shape, jnp.float32) * width * level
    return jnp.minimum(jnp.maximum(array, -most), most).astype(held_as)


def setup_inputs(seed: int = 0) -> dict:
    seeds = jax.random.split(jax.random.key(seed), 6)
    orbitals = scatter_about(seeds[0], (NS, NX, GYZ), 1.0, 6.0, ((0, 16), (1, 2)))
    first_rotation = scatter_about(seeds[1], (NS, NS), NS ** -0.5, 0.75, ((1, 16),))
    second_rotation = scatter_about(seeds[2], (NS, NS), NS ** -0.5, 0.75, ((1, 16),))
    occupancy = draw_occupancy(jax.random.fold_in(seeds[5], 71), 0)
    local_potential = jnp.clip(-2.0 + 2.5 * jax.random.uniform(seeds[4], (NX, GYZ), jnp.float32) ** block_levels(seeds[4], (NX, GYZ), ((0, 2),), -0.2, 0.2), -2.0, 0.5)
    return {"orbitals": orbitals, "first_rotation": first_rotation, "second_rotation": second_rotation, "occupancy": occupancy, "local_potential": local_potential}


stencil_weights = (-5369.0 / 1800.0, 12.0 / 7.0, -15.0 / 56.0, 10.0 / 189.0, -1.0 / 112.0, 2.0 / 1925.0, -1.0 / 16632.0)
kinetic_scale = -0.5 / 2.25
exchange_scale = -0.98474502184269641


def second_difference(inner_field, axis_number):
    length = inner_field.shape[axis_number]
    widths = [(0, 0)] * inner_field.ndim
    widths[axis_number] = (RADIUS, RADIUS)
    padded = jnp.pad(inner_field, widths)
    result = stencil_weights[0] * inner_field
    for reach in range(1, RADIUS + 1):
        upper = lax.slice_in_dim(padded, RADIUS + reach, RADIUS + reach + length, axis=axis_number)
        lower = lax.slice_in_dim(padded, RADIUS - reach, RADIUS - reach + length, axis=axis_number)
        result = result + stencil_weights[reach] * (upper + lower)
    return result


def reference(orbitals, first_rotation, second_rotation, occupancy, local_potential):
    flat_rows = orbitals.reshape(NS, NX * GYZ)
    rotated = jnp.dot(first_rotation.T, flat_rows, preferred_element_type=jnp.float32).astype(jnp.bfloat16)
    rotated_wide = rotated.astype(jnp.float32)
    density = jnp.sum(occupancy.astype(jnp.float32)[:, None] * rotated_wide * rotated_wide, axis=0) / NS
    potential = local_potential.reshape(NX * GYZ) + exchange_scale * jnp.cbrt(density + 1e-6)
    potential_grid = potential.reshape(NX, GY, GZ)

    def one_state(state_row):
        inner_field = state_row.astype(jnp.float32).reshape(NX, GY, GZ)
        laplace = second_difference(inner_field, 0) + second_difference(inner_field, 1) + second_difference(inner_field, 2)
        return (kinetic_scale * laplace + potential_grid * inner_field).reshape(NX * GYZ).astype(jnp.bfloat16)

    images = lax.map(one_state, rotated)
    new_images = jnp.dot(second_rotation.T, images, preferred_element_type=jnp.float32).astype(jnp.bfloat16)
    return new_images.reshape(NS, NX, GYZ), density.reshape(NX, GYZ)
```

```python
import functools
import jax
import jax.numpy as jnp
import numpy as np
from jax import lax
from jax.experimental import pallas as pl
from jax.experimental.pallas import tpu as pltpu
from jax.sharding import PartitionSpec as P

GZ = 16
RADIUS = 6
LANES = 128
HALO = 8

stencil_weights = (
    -5369.0 / 1800.0,
    12.0 / 7.0,
    -15.0 / 56.0,
    10.0 / 189.0,
    -1.0 / 112.0,
    2.0 / 1925.0,
    -1.0 / 16632.0,
)
kinetic_scale = -0.5 / 2.25
exchange_scale = -0.9847450218426964

F32 = jnp.float32
BF16 = jnp.bfloat16


def high_low(matrix):
    high = matrix.astype(np.float32).astype(jnp.bfloat16)
    low = (matrix - high.astype(np.float64)).astype(np.float32).astype(jnp.bfloat16)
    return np.stack([high, low])


def plane_matrix(width):
    matrix = np.zeros((width + 2 * LANES, width))
    for c in range(width):
        matrix[LANES + c, c] += 2.0 * stencil_weights[0]
        for reach in range(1, RADIUS + 1):
            for sign in (-1, 1):
                matrix[LANES + c + sign * reach * GZ, c] += stencil_weights[reach]
                if 0 <= c % GZ + sign * reach < GZ:
                    matrix[LANES + c + sign * reach, c] += stencil_weights[reach]
    return high_low(kinetic_scale * matrix)


def first_matrix(states, planes):
    own = states * planes
    matrix = np.zeros((own, own + 2 * states * HALO))
    for s in range(states):
        for p in range(planes):
            for shift in range(-RADIUS, RADIUS + 1):
                q = p + shift
                if q < 0:
                    column = own + s * HALO + HALO + q
                elif q >= planes:
                    column = own + states * HALO + s * HALO + q - planes
                else:
                    column = s * planes + q
                matrix[s * planes + p, column] += stencil_weights[abs(shift)]
    return high_low(kinetic_scale * matrix)


def halo_matrix(states, planes):
    matrix = np.zeros((2, states * HALO, states * planes), np.float32)
    for s in range(states):
        for h in range(HALO):
            matrix[0, s * HALO + h, s * planes + h] = 1.0
            matrix[1, s * HALO + h, s * planes + planes - HALO + h] = 1.0
    return matrix.astype(jnp.bfloat16)


def dot(left, right):
    return jnp.dot(left, right, preferred_element_type=F32)


def kernel(
    n, grids, workers, skip, width, total,
    psi, small, local, ymat, xmat, hmat,
    out, density_out,
    held, smalls, rot1, rot2, sent, phi, density_sent, densities, halo_sent, halos, acc,
    small_send, small_recv, psi_send, psi_recv, phi_send, phi_recv,
    density_send, density_recv, halo_send, halo_recv, own_sem,
):
    me = lax.axis_index("state")
    place = lax.axis_index("grid")
    states, planes = psi.shape[0], psi.shape[1]
    rows = total * planes
    mine = me - skip
    working = jnp.logical_and(mine >= 0, mine < workers)

    def peer(k):
        return lax.rem(me + k, n)

    def is_worker(p):
        return jnp.logical_and(p >= skip, p < skip + workers)

    def lanes(w):
        return pl.ds(pl.multiple_of(w * width, width), width)

    def small_copy(k, p, source):
        return pltpu.make_async_remote_copy(
            src_ref=small, dst_ref=smalls.at[source], send_sem=small_send.at[k],
            recv_sem=small_recv.at[source], device_id={"state": p},
            device_id_type=pl.DeviceIdType.MESH)

    def psi_copy(k, p, w, source):
        return pltpu.make_async_remote_copy(
            src_ref=psi.at[:, :, lanes(w)], dst_ref=held.at[source], send_sem=psi_send.at[k],
            recv_sem=psi_recv.at[source], device_id={"state": p},
            device_id_type=pl.DeviceIdType.MESH)

    def phi_copy(k, p, w):
        return pltpu.make_async_remote_copy(
            src_ref=sent.at[p], dst_ref=phi.at[w + 1], send_sem=phi_send.at[k],
            recv_sem=phi_recv.at[w], device_id={"state": p},
            device_id_type=pl.DeviceIdType.MESH)

    def density_copy(k, p, w):
        return pltpu.make_async_remote_copy(
            src_ref=density_sent, dst_ref=densities.at[w], send_sem=density_send.at[k],
            recv_sem=density_recv.at[w], device_id={"state": p},
            device_id_type=pl.DeviceIdType.MESH)

    def halo_copy(side, w):
        return pltpu.make_async_remote_copy(
            src_ref=halo_sent.at[side, w], dst_ref=halos.at[1 - side, w],
            send_sem=halo_send.at[side, w], recv_sem=halo_recv.at[1 - side, w],
            device_id={"grid": place - 1 if side == 0 else place + 1},
            device_id_type=pl.DeviceIdType.MESH)

    has_low = place > 0
    has_high = place < grids - 1

    barrier = pltpu.get_barrier_semaphore()

    @pl.loop(1, n)
    def _(k):
        pl.semaphore_signal(barrier, inc=1, device_id={"state": peer(k)},
                            device_id_type=pl.DeviceIdType.MESH)

    @pl.when(has_low)
    def _():
        pl.semaphore_signal(barrier, inc=1, device_id={"grid": place - 1},
                            device_id_type=pl.DeviceIdType.MESH)

    @pl.when(has_high)
    def _():
        pl.semaphore_signal(barrier, inc=1, device_id={"grid": place + 1},
                            device_id_type=pl.DeviceIdType.MESH)

    below = (place + grids - 1) // grids
    above = (2 * grids - 2 - place) // grids
    pl.semaphore_wait(barrier, n - 1 + below + above)

    @pl.loop(1, n)
    def _(k):
        p = peer(k)

        @pl.when(is_worker(p))
        def _():
            small_copy(k, p, me).start()

    @pl.loop(1, n)
    def _(k):
        p = peer(k)

        @pl.when(is_worker(p))
        def _():
            psi_copy(k, p, p - skip, me).start()

    phi[0] = jnp.zeros(phi.shape[1:], BF16)
    phi[workers + 1] = jnp.zeros(phi.shape[1:], BF16)

    @pl.when(jnp.logical_not(has_low))
    def _():
        halos[0] = jnp.zeros(halos.shape[1:], BF16)

    @pl.when(jnp.logical_not(has_high))
    def _():
        halos[1] = jnp.zeros(halos.shape[1:], BF16)

    @pl.when(working)
    def _():
        own = pltpu.make_async_copy(psi.at[:, :, lanes(mine)], held.at[me], own_sem)
        own.start()
        smalls[me] = small[...]

        @pl.loop(1, n)
        def _(k):
            small_copy(k, me, peer(k)).wait_recv()

        matrices = smalls[...].reshape(n * smalls.shape[1], LANES)
        wide = matrices.shape[0]
        row = lax.broadcasted_iota(jnp.int32, (rows, wide), 0)
        column = lax.broadcasted_iota(jnp.int32, (rows, wide), 1)
        base = (row // planes) * 4

        def repeated(which):
            pick = jnp.where(column == base + which, 1.0, 0.0).astype(BF16)
            return dot(pick, matrices)

        part = 2 * LANES
        keep = (lax.broadcasted_iota(jnp.int32, (rows, part), 0) % planes
                == lax.broadcasted_iota(jnp.int32, (rows, part), 1) % planes)
        for which, target in ((0, rot1), (1, rot2)):
            tall = repeated(which).astype(BF16)

            @pl.loop(0, rows // part)
            def _(c):
                entry = lax.broadcasted_iota(jnp.int32, (LANES, part), 0)
                at = (lax.broadcasted_iota(jnp.int32, (LANES, part), 1) + c * part) // planes
                spread = jnp.where(entry == at, 1.0, 0.0).astype(BF16)
                target[:, pl.ds(pl.multiple_of(c * part, part), part)] = jnp.where(
                    keep, dot(tall, spread), 0.0).astype(BF16)

        occupied = repeated(2)
        own.wait()

        @pl.loop(1, n)
        def _(k):
            psi_copy(k, me, mine, peer(k)).wait_recv()

        rotated = dot(rot1[...], held[...].reshape(rows, width)).astype(BF16)
        weight = jnp.concatenate([occupied] * (width // LANES), axis=1)
        squares = rotated.astype(F32)
        squares = weight * squares * squares
        density = jnp.sum(squares.reshape(total, planes, width), axis=0) / total
        density_sent[...] = density.astype(BF16)

        sent[...] = dot(rot2[...], rotated).astype(BF16).reshape(sent.shape)

        @pl.loop(1, n)
        def _(k):
            phi_copy(k, peer(k), mine).start()

        @pl.loop(1, n)
        def _(k):
            density_copy(k, peer(k), mine).start()

        phi[mine + 1] = sent[me]
        densities[mine] = density_sent[...]

    @pl.loop(0, workers)
    def _(j):
        w = lax.rem(mine + j + workers, workers)

        @pl.when(w != mine)
        def _():
            phi_copy(0, me, w).wait_recv()

        block = phi[w + 1].reshape(states * planes, width)

        @pl.when(has_low)
        def _():
            halo_sent[0, w] = dot(hmat[0], block).astype(BF16)
            halo_copy(0, w).start()

        @pl.when(has_high)
        def _():
            halo_sent[1, w] = dot(hmat[1], block).astype(BF16)
            halo_copy(1, w).start()

    flat = (workers * states * planes, -1)
    side = jnp.concatenate(
        [
            phi[0:workers, :, :, width - LANES:].reshape(flat[0], LANES),
            phi[1:workers + 1].reshape(flat[0], width),
            phi[2:workers + 2, :, :, :LANES].reshape(flat[0], LANES),
        ],
        axis=1,
    )
    acc[...] = (dot(side, ymat[0]) + dot(side, ymat[1])).reshape(acc.shape)

    @pl.loop(0, workers)
    def _(w):
        @pl.when(w != mine)
        def _():
            density_copy(0, me, w).wait_recv()

        @pl.when(has_low)
        def _():
            halo_copy(1, w).wait_recv()

        @pl.when(has_high)
        def _():
            halo_copy(0, w).wait_recv()

        density = densities[w].astype(F32)
        density_out[:, lanes(w)] = density
        potential = local[:, lanes(w)] + exchange_scale * jnp.exp(
            jnp.log(density + 1e-06) * (1.0 / 3.0))
        block = phi[w + 1]
        column = jnp.concatenate(
            [block.reshape(states * planes, width), halos[0, w], halos[1, w]], axis=0)
        kinetic = acc[w] + dot(xmat[0], column) + dot(xmat[1], column)
        result = kinetic.reshape(states, planes, width) + potential[None] * block.astype(F32)
        out[:, :, lanes(w)] = result.astype(BF16)

    @pl.loop(1, n)
    def _(k):
        p = peer(k)

        @pl.when(is_worker(p))
        def _():
            small_copy(k, p, me).wait_send()
            psi_copy(k, p, p - skip, me).wait_send()

        @pl.when(working)
        def _():
            phi_copy(k, p, mine).wait_send()
            density_copy(k, p, mine).wait_send()

    @pl.loop(0, workers)
    def _(w):
        @pl.when(has_low)
        def _():
            halo_copy(0, w).wait_send()

        @pl.when(has_high)
        def _():
            halo_copy(1, w).wait_send()


def on_device(n, grids, orbitals, first_rotation, second_rotation, occupancy, local_potential):
    states, planes, row_length = orbitals.shape
    total = first_rotation.shape[0]
    width = LANES * (-(-row_length // (LANES * n)))
    workers = row_length // width
    skip = (n - workers) // 2
    pad = ((0, 0), (0, LANES - total))
    small = jnp.stack(
        [
            jnp.pad(first_rotation.T, pad),
            jnp.pad(second_rotation.T, pad),
            jnp.broadcast_to(occupancy[:, None], (states, LANES)),
            jnp.zeros((states, LANES), BF16),
        ],
        axis=1,
    ).reshape(4 * states, LANES)
    ymat = jnp.asarray(plane_matrix(width))
    xmat = jnp.asarray(first_matrix(states, planes))
    hmat = jnp.asarray(halo_matrix(states, planes))
    vmem = pl.BlockSpec(memory_space=pltpu.VMEM)
    rows = total * planes
    dma = pltpu.SemaphoreType.DMA
    return pl.pallas_call(
        functools.partial(kernel, n, grids, workers, skip, width, total),
        out_shape=(
            jax.ShapeDtypeStruct(orbitals.shape, BF16),
            jax.ShapeDtypeStruct(local_potential.shape, F32),
        ),
        in_specs=[pl.BlockSpec(memory_space=pl.ANY)] + [vmem] * 5,
        out_specs=(vmem, vmem),
        scratch_shapes=[
            pltpu.VMEM((n, states, planes, width), BF16),
            pltpu.VMEM((n, 4 * states, LANES), BF16),
            pltpu.VMEM((rows, rows), BF16),
            pltpu.VMEM((rows, rows), BF16),
            pltpu.VMEM((n, states, planes, width), BF16),
            pltpu.VMEM((workers + 2, states, planes, width), BF16),
            pltpu.VMEM((planes, width), BF16),
            pltpu.VMEM((workers, planes, width), BF16),
            pltpu.VMEM((2, workers, states * HALO, width), BF16),
            pltpu.VMEM((2, workers, states * HALO, width), BF16),
            pltpu.VMEM((workers, states * planes, width), F32),
            dma((n,)), dma((n,)), dma((n,)), dma((n,)),
            dma((n,)), dma((workers,)), dma((n,)), dma((workers,)),
            dma((2, workers)), dma((2, workers)), dma,
        ],
        compiler_params=pltpu.CompilerParams(
            collective_id=0, has_side_effects=True, vmem_limit_bytes=56 * 1024 * 1024
        ),
        cost_estimate=pl.CostEstimate(
            flops=3_000_000_000, bytes_accessed=4_000_000, transcendentals=120_000),
    )(orbitals, small, local_potential, ymat, xmat, hmat)


def solution(mesh):
    placed = (
        P("state", "grid", None),
        P(None, "state"),
        P(None, "state"),
        P("state"),
        P("grid", None),
    )
    return jax.shard_map(
        functools.partial(on_device, mesh.shape["state"], mesh.shape["grid"]),
        mesh=mesh,
        in_specs=placed,
        out_specs=(P("state", "grid", None), P("grid", None)),
        check_vma=False,
    )
```

```python
import functools
import jax
import jax.numpy as jnp
import numpy as np
from jax import lax
from jax.experimental import pallas as pl
from jax.experimental.pallas import tpu as pltpu
from jax.sharding import PartitionSpec as P

GZ = 16
RADIUS = 6
LANES = 128
HALO = 8

stencil_weights = (
    -5369.0 / 1800.0,
    12.0 / 7.0,
    -15.0 / 56.0,
    10.0 / 189.0,
    -1.0 / 112.0,
    2.0 / 1925.0,
    -1.0 / 16632.0,
)
kinetic_scale = -0.5 / 2.25
exchange_scale = -0.9847450218426964

F32 = jnp.float32
BF16 = jnp.bfloat16


def high_low(matrix):
    high = matrix.astype(np.float32).astype(jnp.bfloat16)
    low = (matrix - high.astype(np.float64)).astype(np.float32).astype(jnp.bfloat16)
    return np.stack([high, low])


def plane_matrix():
    matrix = np.zeros((3 * LANES, LANES))
    for c in range(LANES):
        matrix[LANES + c, c] += 2.0 * stencil_weights[0]
        for reach in range(1, RADIUS + 1):
            for sign in (-1, 1):
                matrix[LANES + c + sign * reach * GZ, c] += stencil_weights[reach]
                if 0 <= c % GZ + sign * reach < GZ:
                    matrix[LANES + c + sign * reach, c] += stencil_weights[reach]
    return np.concatenate(list(high_low(kinetic_scale * matrix)), axis=1)


def first_matrix(states, planes):
    own = states * planes
    matrix = np.zeros((own, own + 2 * states * HALO))
    for s in range(states):
        for p in range(planes):
            for shift in range(-RADIUS, RADIUS + 1):
                q = p + shift
                if q < 0:
                    column = own + s * HALO + HALO + q
                elif q >= planes:
                    column = own + states * HALO + s * HALO + q - planes
                else:
                    column = s * planes + q
                matrix[s * planes + p, column] += stencil_weights[abs(shift)]
    return np.concatenate(list(high_low(kinetic_scale * matrix)), axis=0)


def halo_matrix(states, planes):
    matrix = np.zeros((2, states * HALO, states * planes), np.float32)
    for s in range(states):
        for h in range(HALO):
            matrix[0, s * HALO + h, s * planes + h] = 1.0
            matrix[1, s * HALO + h, s * planes + planes - HALO + h] = 1.0
    return matrix.astype(jnp.bfloat16)


def dot(left, right):
    return jnp.dot(left, right, preferred_element_type=F32)


def kernel(
    n, grids, workers, skip, width, total,
    psi, small, local, ymat, xmat, hmat,
    out, density_out,
    held, smalls, rot1, rot2, sent, phi, density_sent, densities, halo_sent, halos, acc,
    small_send, small_recv, psi_send, psi_recv, phi_send, phi_recv,
    density_send, density_recv, halo_send, halo_recv, own_sem,
):
    me = lax.axis_index("state")
    place = lax.axis_index("grid")
    states, planes = psi.shape[0], psi.shape[1]
    rows = total * planes
    mine = me - skip
    working = jnp.logical_and(mine >= 0, mine < workers)

    def peer(k):
        return lax.rem(me + k, n)

    def is_worker(p):
        return jnp.logical_and(p >= skip, p < skip + workers)

    parts = width // LANES
    blocks = workers * parts

    def lanes(w):
        return pl.ds(pl.multiple_of(w * width, width), width)

    def small_copy(k, p, source):
        return pltpu.make_async_remote_copy(
            src_ref=small, dst_ref=smalls.at[source], send_sem=small_send.at[k],
            recv_sem=small_recv.at[source], device_id={"state": p},
            device_id_type=pl.DeviceIdType.MESH)

    def psi_block(w, h):
        return psi.at[:, :, pl.ds(pl.multiple_of(w * width + h * LANES, LANES), LANES)]

    def psi_copy(k, p, w, source, h):
        return pltpu.make_async_remote_copy(
            src_ref=psi_block(w, h), dst_ref=held.at[h, source], send_sem=psi_send.at[h, k],
            recv_sem=psi_recv.at[h, source], device_id={"state": p},
            device_id_type=pl.DeviceIdType.MESH)

    def phi_copy(k, p, w, h):
        return pltpu.make_async_remote_copy(
            src_ref=sent.at[h, p], dst_ref=phi.at[w * parts + h + 1],
            send_sem=phi_send.at[h, k], recv_sem=phi_recv.at[h, w], device_id={"state": p},
            device_id_type=pl.DeviceIdType.MESH)

    def density_copy(k, p, w):
        return pltpu.make_async_remote_copy(
            src_ref=density_sent, dst_ref=densities.at[w], send_sem=density_send.at[k],
            recv_sem=density_recv.at[w], device_id={"state": p},
            device_id_type=pl.DeviceIdType.MESH)

    def halo_copy(side, h):
        return pltpu.make_async_remote_copy(
            src_ref=halo_sent.at[side, h], dst_ref=halos.at[1 - side, h],
            send_sem=halo_send.at[side, h], recv_sem=halo_recv.at[1 - side, h],
            device_id={"grid": place - 1 if side == 0 else place + 1},
            device_id_type=pl.DeviceIdType.MESH)

    has_low = place > 0
    has_high = place < grids - 1

    barrier = pltpu.get_barrier_semaphore()

    @pl.loop(1, n)
    def _(k):
        pl.semaphore_signal(barrier, inc=1, device_id={"state": peer(k)},
                            device_id_type=pl.DeviceIdType.MESH)

    @pl.when(has_low)
    def _():
        pl.semaphore_signal(barrier, inc=1, device_id={"grid": place - 1},
                            device_id_type=pl.DeviceIdType.MESH)

    @pl.when(has_high)
    def _():
        pl.semaphore_signal(barrier, inc=1, device_id={"grid": place + 1},
                            device_id_type=pl.DeviceIdType.MESH)

    below = (place + grids - 1) // grids
    above = (2 * grids - 2 - place) // grids
    pl.semaphore_wait(barrier, n - 1 + below + above)

    @pl.loop(1, n)
    def _(k):
        p = peer(k)

        @pl.when(is_worker(p))
        def _():
            small_copy(k, p, me).start()

    for h in range(parts):
        @pl.loop(1, n)
        def _(k):
            p = peer(k)

            @pl.when(is_worker(p))
            def _():
                psi_copy(k, p, p - skip, me, h).start()

    phi[0] = jnp.zeros(phi.shape[1:], BF16)
    phi[blocks + 1] = jnp.zeros(phi.shape[1:], BF16)

    @pl.when(jnp.logical_not(has_low))
    def _():
        halos[0] = jnp.zeros(halos.shape[1:], BF16)

    @pl.when(jnp.logical_not(has_high))
    def _():
        halos[1] = jnp.zeros(halos.shape[1:], BF16)

    @pl.when(working)
    def _():
        owns = [
            pltpu.make_async_copy(psi_block(mine, h), held.at[h, me], own_sem.at[h])
            for h in range(parts)
        ]
        for own in owns:
            own.start()
        smalls[me] = small[...]

        @pl.loop(1, n)
        def _(k):
            small_copy(k, me, peer(k)).wait_recv()

        matrices = smalls[...].reshape(n * smalls.shape[1], LANES)
        wide = matrices.shape[0]
        row = lax.broadcasted_iota(jnp.int32, (rows, wide), 0)
        column = lax.broadcasted_iota(jnp.int32, (rows, wide), 1)
        base = (row // planes) * 4

        def repeated(which):
            pick = jnp.where(column == base + which, 1.0, 0.0).astype(BF16)
            return dot(pick, matrices)

        part = 2 * LANES
        keep = (lax.broadcasted_iota(jnp.int32, (rows, part), 0) % planes
                == lax.broadcasted_iota(jnp.int32, (rows, part), 1) % planes)
        for which, target in ((0, rot1), (1, rot2)):
            tall = repeated(which).astype(BF16)

            @pl.loop(0, rows // part)
            def _(c):
                entry = lax.broadcasted_iota(jnp.int32, (LANES, part), 0)
                at = (lax.broadcasted_iota(jnp.int32, (LANES, part), 1) + c * part) // planes
                spread = jnp.where(entry == at, 1.0, 0.0).astype(BF16)
                target[:, pl.ds(pl.multiple_of(c * part, part), part)] = jnp.where(
                    keep, dot(tall, spread), 0.0).astype(BF16)

        occupied = repeated(2)
        for h in range(parts):
            owns[h].wait()

            @pl.loop(1, n)
            def _(k):
                psi_copy(k, me, mine, peer(k), h).wait_recv()

            rotated = dot(rot1[...], held[h].reshape(rows, LANES)).astype(BF16)
            sent[h] = dot(rot2[...], rotated).astype(BF16).reshape(sent.shape[1:])

            @pl.loop(1, n)
            def _(k):
                phi_copy(k, peer(k), mine, h).start()

            squares = rotated.astype(F32)
            squares = occupied * squares * squares
            density = jnp.sum(squares.reshape(total, planes, LANES), axis=0) / total
            density_sent[:, h * LANES:(h + 1) * LANES] = density.astype(BF16)
            phi[mine * parts + h + 1] = sent[h, me]

        @pl.loop(1, n)
        def _(k):
            density_copy(k, peer(k), mine).start()

        densities[mine] = density_sent[...]

    own_rows = states * planes
    for h in range(parts):
        @pl.loop(0, workers)
        def _(w):
            @pl.when(w != mine)
            def _():
                phi_copy(0, me, w, h).wait_recv()

        for side, present in ((0, has_low), (1, has_high)):
            @pl.when(present)
            def _():
                half = jnp.concatenate(
                    [phi[w * parts + h + 1].reshape(own_rows, LANES) for w in range(workers)],
                    axis=1)
                outer = dot(hmat[side], half).astype(BF16)
                for w in range(workers):
                    halo_sent[side, h, w] = outer[:, w * LANES:(w + 1) * LANES]
                halo_copy(side, h).start()

    @pl.loop(0, workers)
    def _(w):
        @pl.when(w != mine)
        def _():
            density_copy(0, me, w).wait_recv()

    group = 2
    span = group * parts

    @pl.loop(0, workers // group)
    def _(g):
        first = g * span
        side = jnp.concatenate(
            [phi[pl.ds(first + shift, span)].reshape(span * own_rows, LANES)
             for shift in range(3)], axis=1)
        both = dot(side, ymat[...])
        both = (both[:, :LANES] + both[:, LANES:]).reshape(span, own_rows, LANES)
        kinetic = jnp.concatenate([both[i] for i in range(span)], axis=1)
        middle = phi[pl.ds(first + 1, span)].reshape(span, own_rows, LANES)
        block = jnp.concatenate([middle[i] for i in range(span)], axis=1)
        across = dot(xmat[:, :own_rows], block)
        kinetic = kinetic + (across[:own_rows] + across[own_rows:])
        arrived = densities[pl.ds(g * group, group)]
        density = jnp.concatenate([arrived[i] for i in range(group)], axis=1).astype(F32)
        at = pl.ds(pl.multiple_of(g * span * LANES, span * LANES), span * LANES)
        density_out[:, at] = density
        potential = local[:, at] + exchange_scale * jnp.exp(
            jnp.log(density + 1e-06) * (1.0 / 3.0))
        acc[g] = kinetic.reshape(states, planes, span * LANES) + (
            potential[None] * block.astype(F32).reshape(states, planes, span * LANES))

    for h in range(parts):
        @pl.when(has_low)
        def _():
            halo_copy(1, h).wait_recv()

        @pl.when(has_high)
        def _():
            halo_copy(0, h).wait_recv()

    @pl.loop(0, workers // group)
    def _(g):
        outer = jnp.concatenate(
            [jnp.concatenate([halos[0, h, g * group + i], halos[1, h, g * group + i]], axis=0)
             for i in range(group) for h in range(parts)], axis=1)
        across = dot(xmat[:, own_rows:], outer)
        across = (across[:own_rows] + across[own_rows:]).reshape(
            states, planes, span * LANES)
        at = pl.ds(pl.multiple_of(g * span * LANES, span * LANES), span * LANES)
        out[:, :, at] = (acc[g] + across).astype(BF16)

    @pl.loop(1, n)
    def _(k):
        p = peer(k)

        @pl.when(is_worker(p))
        def _():
            small_copy(k, p, me).wait_send()
            for h in range(parts):
                psi_copy(k, p, p - skip, me, h).wait_send()

        @pl.when(working)
        def _():
            for h in range(parts):
                phi_copy(k, p, mine, h).wait_send()
            density_copy(k, p, mine).wait_send()

    for h in range(parts):
        @pl.when(has_low)
        def _():
            halo_copy(0, h).wait_send()

        @pl.when(has_high)
        def _():
            halo_copy(1, h).wait_send()


def on_device(n, grids, orbitals, first_rotation, second_rotation, occupancy, local_potential):
    states, planes, row_length = orbitals.shape
    total = first_rotation.shape[0]
    width = LANES * (-(-row_length // (LANES * n)))
    workers = row_length // width
    parts = width // LANES
    skip = (n - workers) // 2
    pad = ((0, 0), (0, LANES - total))
    small = jnp.stack(
        [
            jnp.pad(first_rotation.T, pad),
            jnp.pad(second_rotation.T, pad),
            jnp.broadcast_to(occupancy[:, None], (states, LANES)),
            jnp.zeros((states, LANES), BF16),
        ],
        axis=1,
    ).reshape(4 * states, LANES)
    ymat = jnp.asarray(plane_matrix())
    xmat = jnp.asarray(first_matrix(states, planes))
    hmat = jnp.asarray(halo_matrix(states, planes))
    vmem = pl.BlockSpec(memory_space=pltpu.VMEM)
    rows = total * planes
    dma = pltpu.SemaphoreType.DMA
    return pl.pallas_call(
        functools.partial(kernel, n, grids, workers, skip, width, total),
        out_shape=(
            jax.ShapeDtypeStruct(orbitals.shape, BF16),
            jax.ShapeDtypeStruct(local_potential.shape, F32),
        ),
        in_specs=[pl.BlockSpec(memory_space=pl.ANY)] + [vmem] * 5,
        out_specs=(vmem, vmem),
        scratch_shapes=[
            pltpu.VMEM((parts, n, states, planes, LANES), BF16),
            pltpu.VMEM((n, 4 * states, LANES), BF16),
            pltpu.VMEM((rows, rows), BF16),
            pltpu.VMEM((rows, rows), BF16),
            pltpu.VMEM((parts, n, states, planes, LANES), BF16),
            pltpu.VMEM((workers * parts + 2, states, planes, LANES), BF16),
            pltpu.VMEM((planes, width), BF16),
            pltpu.VMEM((workers, planes, width), BF16),
            pltpu.VMEM((2, parts, workers, states * HALO, LANES), BF16),
            pltpu.VMEM((2, parts, workers, states * HALO, LANES), BF16),
            pltpu.VMEM((workers // 2, states, planes, 2 * width), F32),
            dma((n,)), dma((n,)), dma((parts, n)), dma((parts, n)),
            dma((parts, n)), dma((parts, workers)), dma((n,)), dma((workers,)),
            dma((2, parts)), dma((2, parts)), dma((parts,)),
        ],
        compiler_params=pltpu.CompilerParams(
            collective_id=0, has_side_effects=True, vmem_limit_bytes=56 * 1024 * 1024
        ),
        cost_estimate=pl.CostEstimate(
            flops=3_000_000_000, bytes_accessed=4_000_000, transcendentals=120_000),
    )(orbitals, small, local_potential, ymat, xmat, hmat)


def solution(mesh):
    placed = (
        P("state", "grid", None),
        P(None, "state"),
        P(None, "state"),
        P("state"),
        P("grid", None),
    )
    return jax.shard_map(
        functools.partial(on_device, mesh.shape["state"], mesh.shape["grid"]),
        mesh=mesh,
        in_specs=placed,
        out_specs=(P("state", "grid", None), P("grid", None)),
        check_vma=False,
    )
```

```python
import functools
import jax
import jax.numpy as jnp
import numpy as np
from jax import lax
from jax.experimental import pallas as pl
from jax.experimental.pallas import tpu as pltpu
from jax.sharding import PartitionSpec as P

GZ = 16
RADIUS = 6
LANES = 128
HALO = 8

stencil_weights = (
    -5369.0 / 1800.0,
    12.0 / 7.0,
    -15.0 / 56.0,
    10.0 / 189.0,
    -1.0 / 112.0,
    2.0 / 1925.0,
    -1.0 / 16632.0,
)
kinetic_scale = -0.5 / 2.25
exchange_scale = -0.9847450218426964

F32 = jnp.float32
BF16 = jnp.bfloat16


def high_low(matrix):
    high = matrix.astype(np.float32).astype(jnp.bfloat16)
    low = (matrix - high.astype(np.float64)).astype(np.float32).astype(jnp.bfloat16)
    return np.stack([high, low])


def plane_matrix():
    matrix = np.zeros((3 * LANES, LANES))
    for c in range(LANES):
        matrix[LANES + c, c] += 2.0 * stencil_weights[0]
        for reach in range(1, RADIUS + 1):
            for sign in (-1, 1):
                matrix[LANES + c + sign * reach * GZ, c] += stencil_weights[reach]
                if 0 <= c % GZ + sign * reach < GZ:
                    matrix[LANES + c + sign * reach, c] += stencil_weights[reach]
    return np.concatenate(list(high_low(kinetic_scale * matrix)), axis=1)


def first_matrix(states, planes):
    own = states * planes
    matrix = np.zeros((own, own + 2 * states * HALO))
    for s in range(states):
        for p in range(planes):
            for shift in range(-RADIUS, RADIUS + 1):
                q = p + shift
                if q < 0:
                    column = own + s * HALO + HALO + q
                elif q >= planes:
                    column = own + states * HALO + s * HALO + q - planes
                else:
                    column = s * planes + q
                matrix[s * planes + p, column] += stencil_weights[abs(shift)]
    return np.concatenate(list(high_low(kinetic_scale * matrix)), axis=0)


def halo_matrix(states, planes):
    matrix = np.zeros((2, states * HALO, states * planes), np.float32)
    for s in range(states):
        for h in range(HALO):
            matrix[0, s * HALO + h, s * planes + h] = 1.0
            matrix[1, s * HALO + h, s * planes + planes - HALO + h] = 1.0
    return matrix.astype(jnp.bfloat16)


def dot(left, right):
    return jnp.dot(left, right, preferred_element_type=F32)


def kernel(
    n, grids, workers, skip, width, total,
    psi, small, local, ymat, xmat, hmat,
    out, density_out,
    held, smalls, rot1, rot2, sent, phi, density_sent, densities, halo_sent, halos, acc,
    small_send, small_recv, psi_send, psi_recv, phi_send, phi_recv,
    density_send, density_recv, forward_send, halo_send, halo_recv, own_sem,
):
    me = lax.axis_index("state")
    place = lax.axis_index("grid")
    states, planes = psi.shape[0], psi.shape[1]
    rows = total * planes
    mine = me - skip
    working = jnp.logical_and(mine >= 0, mine < workers)

    def peer(k):
        return lax.rem(me + k, n)

    def is_worker(p):
        return jnp.logical_and(p >= skip, p < skip + workers)

    parts = width // LANES
    blocks = workers * parts

    def lanes(w):
        return pl.ds(pl.multiple_of(w * width, width), width)

    def small_copy(k, p, source):
        return pltpu.make_async_remote_copy(
            src_ref=small, dst_ref=smalls.at[source], send_sem=small_send.at[k],
            recv_sem=small_recv.at[source], device_id={"state": p},
            device_id_type=pl.DeviceIdType.MESH)

    def psi_block(w, h):
        return psi.at[:, :, pl.ds(pl.multiple_of(w * width + h * LANES, LANES), LANES)]

    def psi_copy(k, p, w, source, h):
        return pltpu.make_async_remote_copy(
            src_ref=psi_block(w, h), dst_ref=held.at[h, source], send_sem=psi_send.at[h, k],
            recv_sem=psi_recv.at[h, source], device_id={"state": p},
            device_id_type=pl.DeviceIdType.MESH)

    def phi_copy(k, p, w, h):
        return pltpu.make_async_remote_copy(
            src_ref=sent.at[h, p], dst_ref=phi.at[w * parts + h + 1],
            send_sem=phi_send.at[h, k], recv_sem=phi_recv.at[h, w], device_id={"state": p},
            device_id_type=pl.DeviceIdType.MESH)

    def density_copy(k, p, w):
        return pltpu.make_async_remote_copy(
            src_ref=density_sent, dst_ref=densities.at[w], send_sem=density_send.at[k],
            recv_sem=density_recv.at[w], device_id={"state": p},
            device_id_type=pl.DeviceIdType.MESH)

    def forward_copy(w):
        return pltpu.make_async_remote_copy(
            src_ref=densities.at[w], dst_ref=densities.at[w], send_sem=forward_send.at[w],
            recv_sem=density_recv.at[w], device_id={"state": me + 1 - 2 * lax.rem(me, 2)},
            device_id_type=pl.DeviceIdType.MESH)

    def same_core(w):
        return lax.rem(w + skip, 2) == lax.rem(me, 2)

    def halo_copy(side, h):
        return pltpu.make_async_remote_copy(
            src_ref=halo_sent.at[side, h], dst_ref=halos.at[1 - side, h],
            send_sem=halo_send.at[side, h], recv_sem=halo_recv.at[1 - side, h],
            device_id={"grid": place - 1 if side == 0 else place + 1},
            device_id_type=pl.DeviceIdType.MESH)

    has_low = place > 0
    has_high = place < grids - 1

    barrier = pltpu.get_barrier_semaphore()

    @pl.loop(1, n)
    def _(k):
        pl.semaphore_signal(barrier, inc=1, device_id={"state": peer(k)},
                            device_id_type=pl.DeviceIdType.MESH)

    @pl.when(has_low)
    def _():
        pl.semaphore_signal(barrier, inc=1, device_id={"grid": place - 1},
                            device_id_type=pl.DeviceIdType.MESH)

    @pl.when(has_high)
    def _():
        pl.semaphore_signal(barrier, inc=1, device_id={"grid": place + 1},
                            device_id_type=pl.DeviceIdType.MESH)

    below = (place + grids - 1) // grids
    above = (2 * grids - 2 - place) // grids
    pl.semaphore_wait(barrier, n - 1 + below + above)

    @pl.loop(1, n)
    def _(k):
        p = peer(k)

        @pl.when(is_worker(p))
        def _():
            small_copy(k, p, me).start()

    for h in range(parts):
        @pl.loop(1, n)
        def _(k):
            p = peer(k)

            @pl.when(is_worker(p))
            def _():
                psi_copy(k, p, p - skip, me, h).start()

    phi[0] = jnp.zeros(phi.shape[1:], BF16)
    phi[blocks + 1] = jnp.zeros(phi.shape[1:], BF16)

    @pl.when(jnp.logical_not(has_low))
    def _():
        halos[0] = jnp.zeros(halos.shape[1:], BF16)

    @pl.when(jnp.logical_not(has_high))
    def _():
        halos[1] = jnp.zeros(halos.shape[1:], BF16)

    @pl.when(working)
    def _():
        owns = [
            pltpu.make_async_copy(psi_block(mine, h), held.at[h, me], own_sem.at[h])
            for h in range(parts)
        ]
        for own in owns:
            own.start()
        smalls[me] = small[...]

        @pl.loop(1, n)
        def _(k):
            small_copy(k, me, peer(k)).wait_recv()

        matrices = smalls[...].reshape(n * smalls.shape[1], LANES)
        wide = matrices.shape[0]
        row = lax.broadcasted_iota(jnp.int32, (rows, wide), 0)
        column = lax.broadcasted_iota(jnp.int32, (rows, wide), 1)
        base = (row // planes) * 4

        def repeated(which):
            pick = jnp.where(column == base + which, 1.0, 0.0).astype(BF16)
            return dot(pick, matrices)

        part = 2 * LANES
        keep = (lax.broadcasted_iota(jnp.int32, (rows, part), 0) % planes
                == lax.broadcasted_iota(jnp.int32, (rows, part), 1) % planes)
        for which, target in ((0, rot1), (1, rot2)):
            tall = repeated(which).astype(BF16)

            @pl.loop(0, rows // part)
            def _(c):
                entry = lax.broadcasted_iota(jnp.int32, (LANES, part), 0)
                at = (lax.broadcasted_iota(jnp.int32, (LANES, part), 1) + c * part) // planes
                spread = jnp.where(entry == at, 1.0, 0.0).astype(BF16)
                target[:, pl.ds(pl.multiple_of(c * part, part), part)] = jnp.where(
                    keep, dot(tall, spread), 0.0).astype(BF16)

        occupied = repeated(2)
        for h in range(parts):
            owns[h].wait()

            @pl.loop(1, n)
            def _(k):
                psi_copy(k, me, mine, peer(k), h).wait_recv()

            rotated = dot(rot1[...], held[h].reshape(rows, LANES)).astype(BF16)
            squares = rotated.astype(F32)
            squares = occupied * squares * squares
            density = jnp.sum(squares.reshape(total, planes, LANES), axis=0) / total
            density_sent[:, h * LANES:(h + 1) * LANES] = density.astype(BF16)
            if h == parts - 1:
                densities[mine] = density_sent[...]

                @pl.loop(1, n // 2)
                def _(k):
                    density_copy(2 * k, peer(2 * k), mine).start()

            sent[h] = dot(rot2[...], rotated).astype(BF16).reshape(sent.shape[1:])

            @pl.loop(1, n)
            def _(k):
                phi_copy(k, peer(k), mine, h).start()

            phi[mine * parts + h + 1] = sent[h, me]

    own_rows = states * planes
    for h in range(parts):
        if h == parts - 1:
            @pl.loop(0, workers)
            def _(w):
                @pl.when(same_core(w))
                def _():
                    @pl.when(w != mine)
                    def _():
                        density_copy(0, me, w).wait_recv()

                    forward_copy(w).start()

        @pl.loop(0, workers)
        def _(w):
            @pl.when(w != mine)
            def _():
                phi_copy(0, me, w, h).wait_recv()

        for side, present in ((0, has_low), (1, has_high)):
            @pl.when(present)
            def _():
                half = jnp.concatenate(
                    [phi[w * parts + h + 1].reshape(own_rows, LANES) for w in range(workers)],
                    axis=1)
                outer = dot(hmat[side], half).astype(BF16)
                for w in range(workers):
                    halo_sent[side, h, w] = outer[:, w * LANES:(w + 1) * LANES]
                halo_copy(side, h).start()

    @pl.loop(0, workers)
    def _(w):
        @pl.when(jnp.logical_not(same_core(w)))
        def _():
            forward_copy(w).wait_recv()

    group = 2
    span = group * parts

    @pl.loop(0, workers // group)
    def _(g):
        first = g * span
        side = jnp.concatenate(
            [phi[pl.ds(first + shift, span)].reshape(span * own_rows, LANES)
             for shift in range(3)], axis=1)
        both = dot(side, ymat[...])
        both = (both[:, :LANES] + both[:, LANES:]).reshape(span, own_rows, LANES)
        kinetic = jnp.concatenate([both[i] for i in range(span)], axis=1)
        middle = phi[pl.ds(first + 1, span)].reshape(span, own_rows, LANES)
        block = jnp.concatenate([middle[i] for i in range(span)], axis=1)
        across = dot(xmat[:, :own_rows], block)
        kinetic = kinetic + (across[:own_rows] + across[own_rows:])
        arrived = densities[pl.ds(g * group, group)]
        density = jnp.concatenate([arrived[i] for i in range(group)], axis=1).astype(F32)
        at = pl.ds(pl.multiple_of(g * span * LANES, span * LANES), span * LANES)
        density_out[:, at] = density
        potential = local[:, at] + exchange_scale * jnp.exp(
            jnp.log(density + 1e-06) * (1.0 / 3.0))
        acc[g] = kinetic.reshape(states, planes, span * LANES) + (
            potential[None] * block.astype(F32).reshape(states, planes, span * LANES))

    for h in range(parts):
        @pl.when(has_low)
        def _():
            halo_copy(1, h).wait_recv()

        @pl.when(has_high)
        def _():
            halo_copy(0, h).wait_recv()

    @pl.loop(0, workers // group)
    def _(g):
        outer = jnp.concatenate(
            [jnp.concatenate([halos[0, h, g * group + i], halos[1, h, g * group + i]], axis=0)
             for i in range(group) for h in range(parts)], axis=1)
        across = dot(xmat[:, own_rows:], outer)
        across = (across[:own_rows] + across[own_rows:]).reshape(
            states, planes, span * LANES)
        at = pl.ds(pl.multiple_of(g * span * LANES, span * LANES), span * LANES)
        out[:, :, at] = (acc[g] + across).astype(BF16)

    @pl.loop(1, n)
    def _(k):
        p = peer(k)

        @pl.when(is_worker(p))
        def _():
            small_copy(k, p, me).wait_send()
            for h in range(parts):
                psi_copy(k, p, p - skip, me, h).wait_send()

        @pl.when(working)
        def _():
            for h in range(parts):
                phi_copy(k, p, mine, h).wait_send()

            @pl.when(lax.rem(k, 2) == 0)
            def _():
                density_copy(k, p, mine).wait_send()

    @pl.loop(0, workers)
    def _(w):
        @pl.when(same_core(w))
        def _():
            forward_copy(w).wait_send()

    for h in range(parts):
        @pl.when(has_low)
        def _():
            halo_copy(0, h).wait_send()

        @pl.when(has_high)
        def _():
            halo_copy(1, h).wait_send()


def on_device(n, grids, orbitals, first_rotation, second_rotation, occupancy, local_potential):
    states, planes, row_length = orbitals.shape
    total = first_rotation.shape[0]
    width = LANES * (-(-row_length // (LANES * n)))
    workers = row_length // width
    parts = width // LANES
    skip = (n - workers) // 2
    pad = ((0, 0), (0, LANES - total))
    small = jnp.stack(
        [
            jnp.pad(first_rotation.T, pad),
            jnp.pad(second_rotation.T, pad),
            jnp.broadcast_to(occupancy[:, None], (states, LANES)),
            jnp.zeros((states, LANES), BF16),
        ],
        axis=1,
    ).reshape(4 * states, LANES)
    ymat = jnp.asarray(plane_matrix())
    xmat = jnp.asarray(first_matrix(states, planes))
    hmat = jnp.asarray(halo_matrix(states, planes))
    vmem = pl.BlockSpec(memory_space=pltpu.VMEM)
    rows = total * planes
    dma = pltpu.SemaphoreType.DMA
    return pl.pallas_call(
        functools.partial(kernel, n, grids, workers, skip, width, total),
        out_shape=(
            jax.ShapeDtypeStruct(orbitals.shape, BF16),
            jax.ShapeDtypeStruct(local_potential.shape, F32),
        ),
        in_specs=[pl.BlockSpec(memory_space=pl.ANY)] + [vmem] * 5,
        out_specs=(vmem, vmem),
        scratch_shapes=[
            pltpu.VMEM((parts, n, states, planes, LANES), BF16),
            pltpu.VMEM((n, 4 * states, LANES), BF16),
            pltpu.VMEM((rows, rows), BF16),
            pltpu.VMEM((rows, rows), BF16),
            pltpu.VMEM((parts, n, states, planes, LANES), BF16),
            pltpu.VMEM((workers * parts + 2, states, planes, LANES), BF16),
            pltpu.VMEM((planes, width), BF16),
            pltpu.VMEM((workers, planes, width), BF16),
            pltpu.VMEM((2, parts, workers, states * HALO, LANES), BF16),
            pltpu.VMEM((2, parts, workers, states * HALO, LANES), BF16),
            pltpu.VMEM((workers // 2, states, planes, 2 * width), F32),
            dma((n,)), dma((n,)), dma((parts, n)), dma((parts, n)),
            dma((parts, n)), dma((parts, workers)), dma((n,)), dma((workers,)), dma((workers,)),
            dma((2, parts)), dma((2, parts)), dma((parts,)),
        ],
        compiler_params=pltpu.CompilerParams(
            collective_id=0, has_side_effects=True, vmem_limit_bytes=56 * 1024 * 1024
        ),
        cost_estimate=pl.CostEstimate(
            flops=3_000_000_000, bytes_accessed=4_000_000, transcendentals=120_000),
    )(orbitals, small, local_potential, ymat, xmat, hmat)


def solution(mesh):
    placed = (
        P("state", "grid", None),
        P(None, "state"),
        P(None, "state"),
        P("state"),
        P("grid", None),
    )
    return jax.shard_map(
        functools.partial(on_device, mesh.shape["state"], mesh.shape["grid"]),
        mesh=mesh,
        in_specs=placed,
        out_specs=(P("state", "grid", None), P("grid", None)),
        check_vma=False,
    )
```
